512 devices in a mesh: dp: 8 (over z), vocab: 64 (over y, x, core).
Axes of the slice: x: 4, y: 8, z: 8, core: 2. Of those that a mesh axis runs over, the one named last changes fastest.
Arguments:
- hidden: bfloat16 [1024, 4096], P('dp'), may hold values from -200 to 200
- head_weight: bfloat16 [4096, 81920], P('dp', 'vocab'), may hold values from -0.25 to 0.25
- teacher_logprobs: bfloat16 [1024, 81920], P(('dp', 'vocab')), may hold values from -16 to 16
- lengths: int32 [16], P('dp'), may hold values from 8 to 64
- seq_weights: float32 [16], P('dp'), may hold values from 0.5 to 2
Outputs:
- grad_hidden: bfloat16 [1024, 4096], P('dp')
- grad_head: bfloat16 [4096, 81920], P('dp', 'vocab')
The draws below stay inside these ranges and needn't reach their ends.
All inputs are finite; a program needn't handle non-finite values.
Results may differ from the reference program's by a relative error of at most 0.0065.
Values may be sent and summed in bfloat16 or wider, within the bound.
No kernel may reach another device: no remote copies, remote signals or barrier semaphores. Data moves between devices by JAX's collectives and lax.ppermute only.
A program may use at most 64 MiB of HBM per device.

```python
import math
import jax
import jax.numpy as jnp
from jax import lax

D = 4096
VOCAB = 81920
SEQ_LEN = 64
SEQS = 16
TOKENS = 1024


def draw_hidden(key, part):
    key = jax.random.fold_in(key, 11)
    first = jax.random.fold_in(key, 0)
    base = jax.random.normal(first, (TOKENS, D), jnp.float32)
    values = jnp.clip(base, -6.0, 6.0)
    return jnp.clip(values, -200.0, 200.0).astype(jnp.bfloat16)


def set_ends(result, own_key, least, largest):
    place = [jax.random.randint(jax.random.fold_in(own_key, axis), (), 0, length) for axis, length in enumerate(result.shape)]
    longest = result.shape.index(max(result.shape))
    neighbour = place[:longest] + [(place[longest] + 1) % result.shape[longest]] + place[longest + 1:]
    return result.at[tuple(place)].set(least).at[tuple(neighbour)].set(largest)


def block_levels(key, shape, shards, smallest, high):
    factor_of, own = 1.0, jax.random.fold_in(key, 6)
    for dim, shards_of in shards:
        steps = jnp.exp(jax.random.uniform(jax.random.fold_in(own, dim), (shards_of,), jnp.float32, smallest / len(shards), high / len(shards)))
        factor_of = factor_of * jnp.repeat(steps, shape[dim] // shards_of).reshape([-1 if axis == dim else 1 for axis in range(len(shape))])
    return factor_of


def gaussian(rng, shape, deviation, most, cuts=(), kind=jnp.bfloat16):
    level = block_levels(rng, shape, cuts, -0.22, 0.18) if cuts else 1.0
    drawn = jax.random.normal(rng, shape, jnp.float32) * deviation * level
    return jnp.minimum(jnp.maximum(drawn, -most), most).astype(kind)


def setup_inputs(seed: int = 0) -> dict:
    key_of = jax.random.split(jax.random.key(seed), 6)
    hidden = draw_hidden(jax.random.fold_in(key_of[5], 71), 0)
    head_weight = gaussian(key_of[1], (D, VOCAB), (D // 9) ** -0.5, 0.25, ((0, 8), (1, 64)))
    teacher_logprobs = gaussian(key_of[2], (TOKENS, VOCAB), 3.0, 16.0, ((0, 512),))
    lengths = set_ends(jax.random.randint(key_of[3], (SEQS,), SEQ_LEN // 8, SEQ_LEN + 1), jax.random.fold_in(key_of[3], 1), SEQ_LEN // 8, SEQ_LEN).astype(jnp.int32)
    seq_weights = jnp.clip(jnp.exp(math.log(2.0) - 1.3862944 * jax.random.uniform(key_of[4], (SEQS,), jnp.float32) ** block_levels(key_of[4], (SEQS,), ((0, 8),), -0.2, 0.2)), 0.5, 2.0)
    return dict(hidden=hidden, head_weight=head_weight, teacher_logprobs=teacher_logprobs, lengths=lengths, seq_weights=seq_weights)


loss_scale = 32.0


def reference(hidden, head_weight, teacher_logprobs, lengths, seq_weights):
    logits = jnp.dot(hidden, head_weight, preferred_element_type=jnp.float32)
    top = jnp.max(logits, axis=1, keepdims=True)
    total = jnp.sum(jnp.exp(logits - top), axis=1, keepdims=True)
    log_probs = logits - top - jnp.log(total)
    probs = jnp.exp(log_probs)
    gap = log_probs - teacher_logprobs.astype(jnp.float32)
    divergence = jnp.sum(probs * gap, axis=1, keepdims=True)
    rows = jnp.arange(TOKENS, dtype=jnp.int32)
    sequence = rows // SEQ_LEN
    position = rows % SEQ_LEN
    weight = jnp.where(position < lengths[sequence], seq_weights[sequence], jnp.float32(0.0))
    grad_logits = (loss_scale * weight[:, None] * probs * (gap - divergence)).astype(jnp.bfloat16)
    grad_hidden = lax.dot_general(grad_logits, head_weight, (((1,), (1,)), ((), ())), preferred_element_type=jnp.float32).astype(jnp.bfloat16)
    grad_head = lax.dot_general(hidden, grad_logits, (((0,), (0,)), ((), ())), preferred_element_type=jnp.float32).astype(jnp.bfloat16)
    return grad_hidden, grad_head
```

```python
import jax
import jax.numpy as jnp
from jax import lax
from jax.sharding import PartitionSpec as P

SEQ_LEN = 64
LOSS_SCALE = 32.0


def pair_groups(n):
    return [[2 * i, 2 * i + 1] for i in range(n // 2)]


def core_groups(n):
    return [[2 * i + c for i in range(n // 2)] for c in range(2)]


def spread(block, groups=None, size=None):
    copies = jnp.broadcast_to(block[None], (size,) + block.shape)
    return lax.all_to_all(copies, "vocab", 0, 0, axis_index_groups=groups)


def hidden_slice(hidden, n_dp, n_v):
    rows, d = hidden.shape
    share = rows // n_v
    mine = lax.dynamic_slice_in_dim(hidden, lax.axis_index("vocab") * share, share, 0)
    mine = mine.reshape(share, n_dp, d // n_dp).transpose(1, 0, 2)
    got = lax.all_to_all(mine, "dp", 0, 0)
    everyone = spread(got, None, n_v)
    return everyone.transpose(1, 0, 2, 3).reshape(n_dp * rows, d // n_dp)


def sum_terms(partial_terms, n_v):
    rows, d = partial_terms.shape
    half, many = d // 2, n_v // 2
    swapped = lax.all_to_all(
        partial_terms.reshape(rows, 2, half).transpose(1, 0, 2), "vocab", 0, 0,
        axis_index_groups=pair_groups(n_v),
    )
    mine = (swapped[0] + swapped[1]).astype(jnp.bfloat16)
    terms = lax.all_to_all(
        mine.reshape(many, rows // many, half), "vocab", 0, 0, axis_index_groups=core_groups(n_v)
    )
    total = jnp.sum(terms.astype(jnp.float32), axis=0).astype(jnp.bfloat16)
    whole = spread(total, core_groups(n_v), many).reshape(rows, half)
    both = spread(whole, pair_groups(n_v), 2)
    return jnp.concatenate([both[0], both[1]], axis=1)


def body(hidden, head_weight, teacher_logprobs, lengths, seq_weights):
    n_dp, n_v = lax.axis_size("dp"), lax.axis_size("vocab")
    full_head = lax.all_gather(head_weight, "dp", axis=0, tiled=True)
    teacher = lax.all_to_all(
        teacher_logprobs, "vocab", split_axis=1, concat_axis=0, tiled=True
    ).astype(jnp.float32)
    slices = hidden_slice(hidden, n_dp, n_v)
    tok_rows = hidden.shape[0]

    rows = jnp.arange(tok_rows, dtype=jnp.int32)
    sequence = rows // SEQ_LEN
    position = rows % SEQ_LEN
    member = sequence[:, None] == jnp.arange(lengths.shape[0], dtype=jnp.int32)[None, :]
    row_length = jnp.sum(jnp.where(member, lengths[None, :], 0), axis=1)
    row_weight = jnp.sum(jnp.where(member, seq_weights[None, :], jnp.float32(0.0)), axis=1)
    weight = jnp.where(position < row_length, row_weight, jnp.float32(0.0))

    logits = jnp.dot(hidden, full_head, preferred_element_type=jnp.float32)
    local_top = jnp.max(logits, axis=1)
    shifted = logits - local_top[:, None]
    expd = jnp.exp(shifted)
    diff = shifted - teacher
    stats = jnp.stack([local_top, jnp.sum(expd, axis=1), jnp.sum(expd * diff, axis=1)])
    every = spread(stats, None, n_v)
    tops, sums, weighteds = every[:, 0], every[:, 1], every[:, 2]
    top = jnp.max(tops, axis=0)
    lower = tops - top[None]
    scale = jnp.exp(lower)
    total = jnp.sum(sums * scale, axis=0)
    weighted = jnp.sum(scale * (weighteds + lower * sums), axis=0)
    own = local_top - top
    factor = LOSS_SCALE * weight * jnp.exp(own) / total
    centre = own - weighted / total
    grad_logits = (factor[:, None] * expd * (diff + centre[:, None])).astype(jnp.bfloat16)

    all_grads = lax.all_gather(grad_logits, "dp", axis=0, tiled=True)
    partial_terms = lax.dot_general(
        grad_logits, full_head, (((1,), (1,)), ((), ())), preferred_element_type=jnp.float32
    )
    grad_hidden = sum_terms(partial_terms, n_v)
    grad_head = lax.dot_general(
        slices, all_grads, (((0,), (0,)), ((), ())), preferred_element_type=jnp.float32
    )
    return grad_hidden, grad_head.astype(jnp.bfloat16)


def solution(mesh):
    placed = (P("dp", None), P("dp", "vocab"), P(("dp", "vocab"), None), P("dp"), P("dp"))
    return jax.shard_map(
        body,
        mesh=mesh,
        in_specs=placed,
        out_specs=(P("dp", None), P("dp", "vocab")),
        check_vma=False,
    )
```

```python
import jax
import jax.numpy as jnp
from jax import lax
from jax.sharding import PartitionSpec as P

SEQ_LEN = 64
LOSS_SCALE = 32.0


def pair_groups(n):
    return [[2 * i, 2 * i + 1] for i in range(n // 2)]


def core_groups(n):
    return [[2 * i + c for i in range(n // 2)] for c in range(2)]


def spread(block, groups=None, size=None):
    copies = jnp.broadcast_to(block[None], (size,) + block.shape)
    return lax.all_to_all(copies, "vocab", 0, 0, axis_index_groups=groups)


def hidden_slice(hidden, n_dp, n_v):
    rows, d = hidden.shape
    share = rows // n_v
    mine = lax.dynamic_slice_in_dim(hidden, lax.axis_index("vocab") * share, share, 0)
    mine = mine.reshape(share, n_dp, d // n_dp).transpose(1, 0, 2)
    got = lax.all_to_all(mine, "dp", 0, 0)
    everyone = spread(got, None, n_v)
    return everyone.transpose(1, 0, 2, 3).reshape(n_dp * rows, d // n_dp)


def ring_blocks(block, n):
    right = [(i, (i + 1) % n) for i in range(n)]
    left = [(i, (i - 1) % n) for i in range(n)]
    half = block.shape[0] // 2
    parts = [block[:half], block[half:]]
    got = {0: list(parts)}
    up, down = list(parts), list(parts)
    for step in range(1, n // 2 + 1):
        last = step == n // 2
        down[0] = lax.ppermute(down[0], "dp", left)
        up[1] = lax.ppermute(up[1], "dp", right)
        if not last:
            down[1] = lax.ppermute(down[1], "dp", left)
            up[0] = lax.ppermute(up[0], "dp", right)
            got[step], got[n - step] = list(down), list(up)
        else:
            got[step] = [down[0], up[1]]
    return [got[k] for k in range(n)]


def sum_terms(partial_terms, n_v, other):
    rows, d = partial_terms.shape
    half, many = d // 2, n_v // 2
    swapped = lax.all_to_all(
        partial_terms.reshape(rows, 2, half).transpose(1, 0, 2), "vocab", 0, 0,
        axis_index_groups=pair_groups(n_v),
    )
    mine = (swapped[0] + swapped[1]).astype(jnp.bfloat16)
    terms = lax.all_to_all(
        mine.reshape(many, rows // many, half), "vocab", 0, 0, axis_index_groups=core_groups(n_v)
    )
    total = jnp.sum(terms.astype(jnp.float32), axis=0).astype(jnp.bfloat16)
    whole = spread(total, core_groups(n_v), many).reshape(rows, half)
    whole, other = lax.optimization_barrier((whole, other))
    both = spread(whole, pair_groups(n_v), 2)
    return jnp.concatenate([both[0], both[1]], axis=1), other


def body(hidden, head_weight, teacher_logprobs, lengths, seq_weights):
    n_dp, n_v = lax.axis_size("dp"), lax.axis_size("vocab")
    blocks = ring_blocks(head_weight, n_dp)
    teacher = lax.all_to_all(
        teacher_logprobs, "vocab", split_axis=1, concat_axis=0, tiled=True
    ).astype(jnp.float32)
    slices = hidden_slice(hidden, n_dp, n_v)
    tok_rows = hidden.shape[0]

    rows = jnp.arange(tok_rows, dtype=jnp.int32)
    sequence = rows // SEQ_LEN
    position = rows % SEQ_LEN
    member = sequence[:, None] == jnp.arange(lengths.shape[0], dtype=jnp.int32)[None, :]
    row_length = jnp.sum(jnp.where(member, lengths[None, :], 0), axis=1)
    row_weight = jnp.sum(jnp.where(member, seq_weights[None, :], jnp.float32(0.0)), axis=1)
    weight = jnp.where(position < row_length, row_weight, jnp.float32(0.0))

    me = lax.axis_index("dp")
    depth = head_weight.shape[0]
    part = depth // 2
    logits = None
    order = [0]
    for k in range(1, n_dp // 2 + 1):
        order += [k] if k == n_dp - k else [k, n_dp - k]
    for k in order:
        if k == n_dp // 2:
            blocks[k][0], slices = lax.optimization_barrier((blocks[k][0], slices))
        place = lax.rem(me + k, n_dp) * depth
        for i in range(2):
            feats = lax.dynamic_slice_in_dim(hidden, place + i * part, part, 1)
            term = jnp.dot(feats, blocks[k][i], preferred_element_type=jnp.float32)
            logits = term if logits is None else logits + term
    local_top = jnp.max(logits, axis=1)
    shifted = logits - local_top[:, None]
    expd = jnp.exp(shifted)
    diff = shifted - teacher
    stats = jnp.stack([local_top, jnp.sum(expd, axis=1), jnp.sum(expd * diff, axis=1)])
    every = spread(stats, None, n_v)
    tops, sums, weighteds = every[:, 0], every[:, 1], every[:, 2]
    top = jnp.max(tops, axis=0)
    lower = tops - top[None]
    scale = jnp.exp(lower)
    total = jnp.sum(sums * scale, axis=0)
    weighted = jnp.sum(scale * (weighteds + lower * sums), axis=0)
    own = local_top - top
    factor = LOSS_SCALE * weight * jnp.exp(own) / total
    centre = own - weighted / total
    grad_logits = (factor[:, None] * expd * (diff + centre[:, None])).astype(jnp.bfloat16)

    all_grads = lax.all_gather(grad_logits, "dp", axis=0, tiled=True)
    partial_terms = jnp.concatenate(
        [
            lax.dot_general(
                grad_logits, piece, (((1,), (1,)), ((), ())), preferred_element_type=jnp.float32
            )
            for pieces in blocks
            for piece in pieces
        ],
        axis=1,
    )
    turned, all_grads = sum_terms(partial_terms, n_v, all_grads)
    grad_hidden = jnp.roll(turned, me * depth, axis=1)
    grad_head = lax.dot_general(
        slices, all_grads, (((0,), (0,)), ((), ())), preferred_element_type=jnp.float32
    )
    return grad_hidden, grad_head.astype(jnp.bfloat16)


def solution(mesh):
    placed = (P("dp", None), P("dp", "vocab"), P(("dp", "vocab"), None), P("dp"), P("dp"))
    return jax.shard_map(
        body,
        mesh=mesh,
        in_specs=placed,
        out_specs=(P("dp", None), P("dp", "vocab")),
        check_vma=False,
    )
```

```python
import jax
import jax.numpy as jnp
from jax import lax
from jax.experimental import pallas as pl
from jax.experimental.pallas import tpu as pltpu
from jax.sharding import PartitionSpec as P

SEQ_LEN = 64
LOSS_SCALE = 32.0


def pair_groups(n):
    return [[2 * i, 2 * i + 1] for i in range(n // 2)]


def core_groups(n):
    return [[2 * i + c for i in range(n // 2)] for c in range(2)]


def spread(block, groups=None, size=None):
    copies = jnp.broadcast_to(block[None], (size,) + block.shape)
    return lax.all_to_all(copies, "vocab", 0, 0, axis_index_groups=groups)


def hidden_share(hidden, n_v):
    share = hidden.shape[0] // n_v
    mine = lax.dynamic_slice_in_dim(hidden, lax.axis_index("vocab") * share, share, 0)
    return lax.all_gather(mine, "dp", axis=0)


def ring_blocks(block, n):
    right = [(i, (i + 1) % n) for i in range(n)]
    left = [(i, (i - 1) % n) for i in range(n)]
    half = block.shape[0] // 2
    parts = [block[:half], block[half:]]
    got = {0: list(parts)}
    up, down = list(parts), list(parts)
    for step in range(1, n // 2 + 1):
        last = step == n // 2
        down[0] = lax.ppermute(down[0], "dp", left)
        up[1] = lax.ppermute(up[1], "dp", right)
        if not last:
            down[1] = lax.ppermute(down[1], "dp", left)
            up[0] = lax.ppermute(up[0], "dp", right)
            got[step], got[n - step] = list(down), list(up)
        else:
            got[step] = [down[0], up[1]]
    return [got[k] for k in range(n)]


def terms_kernel(me_ref, grads_ref, *refs):
    pieces, out_ref = refs[:-1], refs[-1]
    blocks, _, depth = out_ref.shape
    per = len(pieces) // blocks
    part = depth // per
    grads = grads_ref[...]
    for j, piece in enumerate(pieces):
        place = lax.rem(me_ref[0] + j // per, blocks)
        out_ref[place, :, pl.ds(j % per * part, part)] = lax.dot_general(
            grads, piece[...], (((1,), (1,)), ((), ())), preferred_element_type=jnp.float32
        )


def hidden_terms(me, grads, pieces, blocks):
    rows, width = grads.shape
    d = sum(piece.shape[0] for piece in pieces)
    vmem = pl.BlockSpec(memory_space=pltpu.VMEM)
    return pl.pallas_call(
        terms_kernel,
        out_shape=jax.ShapeDtypeStruct((blocks, rows, d // blocks), jnp.float32),
        in_specs=[pl.BlockSpec(memory_space=pltpu.SMEM)] + [vmem] * (1 + len(pieces)),
        out_specs=vmem,
        compiler_params=pltpu.CompilerParams(vmem_limit_bytes=24 * 2**20),
        cost_estimate=pl.CostEstimate(
            flops=2 * rows * d * width, bytes_accessed=2 * d * width + 4 * rows * d, transcendentals=0
        ),
    )(me.reshape(1), grads, *pieces)


def sum_terms(terms, n_v, other):
    blocks, rows, d = terms.shape
    many = n_v // 2
    swapped = lax.all_to_all(
        terms.reshape(2, blocks // 2, rows, d), "vocab", 0, 0, axis_index_groups=pair_groups(n_v)
    )
    mine = (swapped[0] + swapped[1]).astype(jnp.bfloat16)
    mine = mine.reshape(many, blocks // 2 * rows // many, d)
    parts = lax.all_to_all(mine, "vocab", 0, 0, axis_index_groups=core_groups(n_v))
    total = jnp.sum(parts.astype(jnp.float32), axis=0).astype(jnp.bfloat16)
    whole = spread(total, core_groups(n_v), many)
    whole, other = lax.optimization_barrier((whole, other))
    both = spread(whole, pair_groups(n_v), 2)
    return both.reshape(blocks, rows, d), other


def body(hidden, head_weight, teacher_logprobs, lengths, seq_weights):
    n_dp, n_v = lax.axis_size("dp"), lax.axis_size("vocab")
    blocks = ring_blocks(head_weight, n_dp)
    teacher = lax.all_to_all(
        teacher_logprobs, "vocab", split_axis=1, concat_axis=0, tiled=True
    ).astype(jnp.float32)
    share = hidden_share(hidden, n_v)
    tok_rows = hidden.shape[0]

    rows = jnp.arange(tok_rows, dtype=jnp.int32)
    sequence = rows // SEQ_LEN
    position = rows % SEQ_LEN
    member = sequence[:, None] == jnp.arange(lengths.shape[0], dtype=jnp.int32)[None, :]
    row_length = jnp.sum(jnp.where(member, lengths[None, :], 0), axis=1)
    row_weight = jnp.sum(jnp.where(member, seq_weights[None, :], jnp.float32(0.0)), axis=1)
    weight = jnp.where(position < row_length, row_weight, jnp.float32(0.0))

    me = lax.axis_index("dp")
    depth = head_weight.shape[0]
    part = depth // 2
    logits = None
    order = [0]
    for k in range(1, n_dp // 2 + 1):
        order += [k] if k == n_dp - k else [k, n_dp - k]
    for k in order:
        if k == 1:
            blocks[k][0], share = lax.optimization_barrier((blocks[k][0], share))
            share = lax.dynamic_slice_in_dim(share, me * depth, depth, 2)
            slices = lax.all_gather(share, "vocab", axis=0)
        place = lax.rem(me + k, n_dp) * depth
        for i in range(2):
            feats = lax.dynamic_slice_in_dim(hidden, place + i * part, part, 1)
            term = jnp.dot(feats, blocks[k][i], preferred_element_type=jnp.float32)
            logits = term if logits is None else logits + term
    local_top = jnp.max(logits, axis=1)
    shifted = logits - local_top[:, None]
    expd = jnp.exp(shifted)
    diff = shifted - teacher
    stats = jnp.stack([local_top, jnp.sum(expd, axis=1), jnp.sum(expd * diff, axis=1)])
    every = spread(stats, None, n_v)
    tops, sums, weighteds = every[:, 0], every[:, 1], every[:, 2]
    top = jnp.max(tops, axis=0)
    lower = tops - top[None]
    scale = jnp.exp(lower)
    total = jnp.sum(sums * scale, axis=0)
    weighted = jnp.sum(scale * (weighteds + lower * sums), axis=0)
    own = local_top - top
    factor = LOSS_SCALE * weight * jnp.exp(own) / total
    centre = own - weighted / total
    grad_logits = (factor[:, None] * expd * (diff + centre[:, None])).astype(jnp.bfloat16)

    slices, grad_logits = lax.optimization_barrier((slices, grad_logits))
    slices = slices.transpose(1, 0, 2, 3).reshape(n_dp * tok_rows, depth)
    all_grads = lax.all_gather(grad_logits, "dp", axis=0, tiled=True)
    terms = hidden_terms(me, grad_logits, [p for pieces in blocks for p in pieces], n_dp)
    summed, all_grads = sum_terms(terms, n_v, all_grads)
    grad_hidden = jnp.concatenate([summed[k] for k in range(n_dp)], axis=1)
    grad_head = lax.dot_general(
        slices, all_grads, (((0,), (0,)), ((), ())), preferred_element_type=jnp.float32
    )
    return grad_hidden, grad_head.astype(jnp.bfloat16)


def solution(mesh):
    placed = (P("dp", None), P("dp", "vocab"), P(("dp", "vocab"), None), P("dp"), P("dp"))
    return jax.shard_map(
        body,
        mesh=mesh,
        in_specs=placed,
        out_specs=(P("dp", None), P("dp", "vocab")),
        check_vma=False,
    )
```

```python
import jax
import jax.numpy as jnp
from jax import lax
from jax.experimental import pallas as pl
from jax.experimental.pallas import tpu as pltpu
from jax.sharding import PartitionSpec as P

SEQ_LEN = 64
LOSS_SCALE = 32.0
GATHERED = 10
LANES = 128
VMEM = pl.BlockSpec(memory_space=pltpu.VMEM)
HBM = pl.BlockSpec(memory_space=pl.ANY)


def pair_groups(n):
    return [[2 * i, 2 * i + 1] for i in range(n // 2)]


def core_groups(n):
    return [[2 * i + c for i in range(n // 2)] for c in range(2)]


def spread(block, size, groups=None, axis="vocab"):
    copies = jnp.broadcast_to(block[None], (size,) + block.shape)
    return lax.all_to_all(copies, axis, 0, 0, axis_index_groups=groups)


def hidden_share(hidden, n_dp, n_v):
    rows, d = hidden.shape
    share = rows // n_v
    mine = lax.dynamic_slice_in_dim(hidden, lax.axis_index("vocab") * share, share, 0)
    return mine.reshape(share, n_dp, d // n_dp).transpose(1, 0, 2)


def ring_blocks(block, n):
    right = [(i, (i + 1) % n) for i in range(n)]
    left = [(i, (i - 1) % n) for i in range(n)]
    half = block.shape[0] // 2
    got = {0: block}
    up = down = block
    for step in range(1, n // 2):
        down, up = lax.ppermute(down, "dp", left), lax.ppermute(up, "dp", right)
        got[step], got[n - step] = down, up
    got[n // 2] = jnp.concatenate(
        [lax.ppermute(down[:half], "dp", left), lax.ppermute(up[half:], "dp", right)]
    )
    return [got[k] for k in range(n)]


def along_lanes(column, rows):
    return jnp.transpose(jnp.broadcast_to(column, (rows, LANES)))[:1]


def stats_kernel(teacher_ref, logits_ref, out_ref):
    rows = logits_ref.shape[0]
    logits = logits_ref[...]
    top = jnp.max(logits, axis=1, keepdims=True)
    shifted = logits - top
    expd = jnp.exp(shifted)
    total = jnp.sum(expd, axis=1, keepdims=True)
    gaps = expd * (shifted - teacher_ref[...].astype(jnp.float32))
    weighted = jnp.sum(gaps, axis=1, keepdims=True)
    stats = jnp.concatenate([along_lanes(v, rows) for v in (top, total, weighted)], axis=0)
    out_ref[...] = jnp.broadcast_to(stats[None], out_ref.shape)


def grads_kernel(every_ref, weight_ref, teacher_ref, logits_ref, out_ref):
    rows, width = logits_ref.shape
    tops, sums, weighteds = (every_ref[:, i, :] for i in range(3))
    top = jnp.max(tops, axis=0, keepdims=True)
    lower = tops - top
    scale = jnp.exp(lower)
    total = jnp.sum(sums * scale, axis=0, keepdims=True)
    weighted = jnp.sum(scale * (weighteds + lower * sums), axis=0, keepdims=True)
    factor = LOSS_SCALE * weight_ref[...] / total
    top, factor, centre = (
        jnp.transpose(jnp.broadcast_to(v, (LANES, rows))) for v in (top, factor, weighted / total)
    )
    for c in range(width // LANES):
        cols = pl.ds(c * LANES, LANES)
        shifted = logits_ref[:, cols] - top
        gap = shifted - teacher_ref[:, cols].astype(jnp.float32) - centre
        out_ref[:, cols] = (factor * jnp.exp(shifted) * gap).astype(jnp.bfloat16)


def terms_kernel(me_ref, grads_ref, gathered_ref, *refs):
    pieces, (out_ref, held, kept, sems, piece_sems) = refs[:-5], refs[-5:]
    blocks = len(pieces)
    deep = held.shape[1]
    copies = [
        pltpu.make_async_copy(gathered_ref.at[pl.ds(j * deep, deep)], held.at[j], sems.at[j])
        for j in range(blocks)
    ]
    piece_copies = [
        pltpu.make_async_copy(piece, kept.at[j], piece_sems.at[j]) for j, piece in enumerate(pieces)
    ]
    for j in range(blocks):
        copies[j].start()
        piece_copies[j].start()
    grads = grads_ref[...]
    contract = (((1,), (1,)), ((), ()))
    for j in range(blocks):
        copies[j].wait()
        out_ref[j, :, :deep] = lax.dot_general(
            grads, held[j], contract, preferred_element_type=jnp.float32
        )
        piece_copies[j].wait()
        out_ref[lax.rem(me_ref[0] + j, blocks), :, deep:] = lax.dot_general(
            grads, kept[j], contract, preferred_element_type=jnp.float32
        )


def hidden_terms(me, grads, gathered, pieces):
    rows, width = grads.shape
    blocks = len(pieces)
    deep, rest = gathered.shape[0] // blocks, pieces[0].shape[0]
    d = blocks * (deep + rest)
    return pl.pallas_call(
        terms_kernel,
        out_shape=jax.ShapeDtypeStruct((blocks, rows, deep + rest), jnp.float32),
        in_specs=[pl.BlockSpec(memory_space=pltpu.SMEM), VMEM, HBM] + [HBM] * blocks,
        out_specs=VMEM,
        scratch_shapes=[
            pltpu.VMEM((blocks, deep, width), gathered.dtype),
            pltpu.VMEM((blocks, rest, width), gathered.dtype),
            pltpu.SemaphoreType.DMA((blocks,)),
            pltpu.SemaphoreType.DMA((blocks,)),
        ],
        compiler_params=pltpu.CompilerParams(vmem_limit_bytes=56 * 2**20),
        cost_estimate=pl.CostEstimate(
            flops=2 * rows * d * width, bytes_accessed=2 * d * width + 4 * rows * d, transcendentals=0
        ),
    )(me.reshape(1), grads, gathered, *pieces)


def row_kernel(kernel, shape, dtype, *args):
    size = args[-1].size
    return pl.pallas_call(
        kernel,
        out_shape=jax.ShapeDtypeStruct(shape, dtype),
        in_specs=[VMEM] * len(args),
        out_specs=VMEM,
        compiler_params=pltpu.CompilerParams(vmem_limit_bytes=16 * 2**20),
        cost_estimate=pl.CostEstimate(flops=8 * size, bytes_accessed=8 * size, transcendentals=size),
    )(*args)


def sum_terms(terms, n_v):
    blocks, rows, d = terms.shape
    many = n_v // 2
    swapped = lax.all_to_all(
        terms.reshape(2, blocks // 2, rows, d), "vocab", 0, 0, axis_index_groups=pair_groups(n_v)
    )
    mine = (swapped[0] + swapped[1]).astype(jnp.bfloat16)
    mine = mine.reshape(many, blocks // 2 * rows // many, d)
    parts = lax.all_to_all(mine, "vocab", 0, 0, axis_index_groups=core_groups(n_v))
    total = jnp.sum(parts.astype(jnp.float32), axis=0).astype(jnp.bfloat16)
    whole = spread(total, many, core_groups(n_v))
    both = spread(whole, 2, pair_groups(n_v))
    return both.reshape(blocks, rows, d)


def body(hidden, head_weight, teacher_logprobs, lengths, seq_weights):
    n_dp, n_v = lax.axis_size("dp"), lax.axis_size("vocab")
    me = lax.axis_index("dp")
    depth, width = head_weight.shape
    tok_rows = hidden.shape[0]
    deep = depth * GATHERED // 16
    gathered = lax.all_gather(head_weight[:deep], "dp", axis=0, tiled=True)
    pieces = ring_blocks(head_weight[deep:], n_dp)
    teacher = lax.all_to_all(teacher_logprobs, "vocab", split_axis=1, concat_axis=0, tiled=True)
    share = lax.all_to_all(hidden_share(hidden, n_dp, n_v), "dp", 0, 0)
    everyone = spread(share, n_v)

    rows = jnp.arange(tok_rows, dtype=jnp.int32)
    sequence = rows // SEQ_LEN
    position = rows % SEQ_LEN
    member = sequence[:, None] == jnp.arange(lengths.shape[0], dtype=jnp.int32)[None, :]
    row_length = jnp.sum(jnp.where(member, lengths[None, :], 0), axis=1)
    row_weight = jnp.sum(jnp.where(member, seq_weights[None, :], jnp.float32(0.0)), axis=1)
    weight = jnp.where(position < row_length, row_weight, jnp.float32(0.0)).reshape(1, tok_rows)

    features = hidden.reshape(tok_rows, n_dp, depth)
    first = features[:, :, :deep].reshape(tok_rows, n_dp * deep)
    logits = None
    for k in range(n_dp):
        feats = lax.dynamic_slice_in_dim(
            hidden, lax.rem(me + k, n_dp) * depth + deep, depth - deep, 1
        )
        term = jnp.dot(feats, pieces[k], preferred_element_type=jnp.float32)
        logits = term if logits is None else logits + term
    gathered, everyone, teacher, logits, weight, first = lax.optimization_barrier(
        (gathered, everyone, teacher, logits, weight, first)
    )
    logits = logits + jnp.dot(first, gathered, preferred_element_type=jnp.float32)
    stats = row_kernel(stats_kernel, (n_v, 3, tok_rows), jnp.float32, teacher, logits)
    every = lax.all_to_all(stats, "vocab", 0, 0)
    grad_logits = row_kernel(
        grads_kernel, logits.shape, jnp.bfloat16, every, weight, teacher, logits
    )

    everyone, grad_logits = lax.optimization_barrier((everyone, grad_logits))
    slices = everyone.transpose(1, 0, 2, 3).reshape(n_dp * tok_rows, depth)
    all_grads = lax.all_gather(grad_logits, "dp", axis=0, tiled=True)
    summed = sum_terms(hidden_terms(me, grad_logits, gathered, pieces), n_v)
    grad_hidden = jnp.concatenate([summed[k] for k in range(n_dp)], axis=1)
    grad_head = lax.dot_general(
        slices, all_grads, (((0,), (0,)), ((), ())), preferred_element_type=jnp.float32
    )
    return grad_hidden, grad_head.astype(jnp.bfloat16)


def solution(mesh):
    placed = (P("dp", None), P("dp", "vocab"), P(("dp", "vocab"), None), P("dp"), P("dp"))
    return jax.shard_map(
        body,
        mesh=mesh,
        in_specs=placed,
        out_specs=(P("dp", None), P("dp", "vocab")),
        check_vma=False,
    )
```

```python
import jax
import jax.numpy as jnp
from jax import lax
from jax.experimental import pallas as pl
from jax.experimental.pallas import tpu as pltpu
from jax.sharding import PartitionSpec as P

SEQ_LEN = 64
LOSS_SCALE = 32.0
GATHERED = 10
LANES = 128
VMEM = pl.BlockSpec(memory_space=pltpu.VMEM)
HBM = pl.BlockSpec(memory_space=pl.ANY)


def pair_groups(n):
    return [[2 * i, 2 * i + 1] for i in range(n // 2)]


def core_groups(n):
    return [[2 * i + c for i in range(n // 2)] for c in range(2)]


def spread(block, size, groups=None, axis="vocab"):
    copies = jnp.broadcast_to(block[None], (size,) + block.shape)
    return lax.all_to_all(copies, axis, 0, 0, axis_index_groups=groups)


def hidden_share(hidden, n_dp, n_v):
    rows, d = hidden.shape
    share = rows // n_v
    mine = lax.dynamic_slice_in_dim(hidden, lax.axis_index("vocab") * share, share, 0)
    return mine.reshape(share, n_dp, d // n_dp).transpose(1, 0, 2)


def ring_blocks(block, n):
    right = [(i, (i + 1) % n) for i in range(n)]
    left = [(i, (i - 1) % n) for i in range(n)]
    half = block.shape[0] // 2
    got = {0: block}
    up = down = block
    for step in range(1, n // 2):
        down, up = lax.ppermute(down, "dp", left), lax.ppermute(up, "dp", right)
        got[step], got[n - step] = down, up
    got[n // 2] = jnp.concatenate(
        [lax.ppermute(down[:half], "dp", left), lax.ppermute(up[half:], "dp", right)]
    )
    return [got[k] for k in range(n)]


def along_lanes(column, rows):
    return jnp.transpose(jnp.broadcast_to(column, (rows, LANES)))[:1]


def stats_kernel(teacher_ref, logits_ref, out_ref):
    rows = logits_ref.shape[0]
    logits = logits_ref[...]
    top = jnp.max(logits, axis=1, keepdims=True)
    shifted = logits - top
    expd = jnp.exp(shifted)
    total = jnp.sum(expd, axis=1, keepdims=True)
    gaps = expd * (shifted - teacher_ref[...].astype(jnp.float32))
    weighted = jnp.sum(gaps, axis=1, keepdims=True)
    stats = jnp.concatenate([along_lanes(v, rows) for v in (top, total, weighted)], axis=0)
    out_ref[...] = jnp.broadcast_to(stats[None], out_ref.shape)


def grads_kernel(every_ref, weight_ref, teacher_ref, logits_ref, out_ref):
    rows, width = logits_ref.shape
    tops, sums, weighteds = (every_ref[:, i, :] for i in range(3))
    top = jnp.max(tops, axis=0, keepdims=True)
    lower = tops - top
    scale = jnp.exp(lower)
    total = jnp.sum(sums * scale, axis=0, keepdims=True)
    weighted = jnp.sum(scale * (weighteds + lower * sums), axis=0, keepdims=True)
    factor = LOSS_SCALE * weight_ref[...] / total
    top, factor, centre = (
        jnp.transpose(jnp.broadcast_to(v, (LANES, rows))) for v in (top, factor, weighted / total)
    )
    for c in range(width // LANES):
        cols = pl.ds(c * LANES, LANES)
        shifted = logits_ref[:, cols] - top
        gap = shifted - teacher_ref[:, cols].astype(jnp.float32) - centre
        out_ref[:, cols] = (factor * jnp.exp(shifted) * gap).astype(jnp.bfloat16)


def terms_kernel(me_ref, grads_ref, gathered_ref, *refs):
    pieces, (out_ref, head, sems, piece_sems) = refs[:-4], refs[-4:]
    blocks, depth, _ = head.shape
    deep = depth - pieces[0].shape[0]
    piece_copies = [
        pltpu.make_async_copy(
            piece,
            head.at[lax.rem(me_ref[0] + j, blocks), pl.ds(deep, depth - deep)],
            piece_sems.at[j],
        )
        for j, piece in enumerate(pieces)
    ]
    copies = [
        pltpu.make_async_copy(
            gathered_ref.at[pl.ds(j * deep, deep)], head.at[j, pl.ds(0, deep)], sems.at[j]
        )
        for j in range(blocks)
    ]
    for copy in piece_copies + copies:
        copy.start()
    grads = grads_ref[...]
    for copy in piece_copies:
        copy.wait()
    for j, copy in enumerate(copies):
        copy.wait()
        out_ref[j] = lax.dot_general(
            grads, head[j], (((1,), (1,)), ((), ())), preferred_element_type=jnp.float32
        )


def hidden_terms(me, grads, gathered, pieces):
    rows, width = grads.shape
    blocks = len(pieces)
    deep, rest = gathered.shape[0] // blocks, pieces[0].shape[0]
    d = blocks * (deep + rest)
    return pl.pallas_call(
        terms_kernel,
        out_shape=jax.ShapeDtypeStruct((blocks, rows, deep + rest), jnp.float32),
        in_specs=[pl.BlockSpec(memory_space=pltpu.SMEM), VMEM, HBM] + [HBM] * blocks,
        out_specs=VMEM,
        scratch_shapes=[
            pltpu.VMEM((blocks, deep + rest, width), gathered.dtype),
            pltpu.SemaphoreType.DMA((blocks,)),
            pltpu.SemaphoreType.DMA((blocks,)),
        ],
        compiler_params=pltpu.CompilerParams(vmem_limit_bytes=56 * 2**20),
        cost_estimate=pl.CostEstimate(
            flops=2 * rows * d * width, bytes_accessed=2 * d * width + 4 * rows * d, transcendentals=0
        ),
    )(me.reshape(1), grads, gathered, *pieces)


def row_kernel(kernel, shape, dtype, *args):
    size = args[-1].size
    return pl.pallas_call(
        kernel,
        out_shape=jax.ShapeDtypeStruct(shape, dtype),
        in_specs=[VMEM] * len(args),
        out_specs=VMEM,
        compiler_params=pltpu.CompilerParams(vmem_limit_bytes=16 * 2**20),
        cost_estimate=pl.CostEstimate(flops=8 * size, bytes_accessed=8 * size, transcendentals=size),
    )(*args)


def sum_terms(terms, n_v):
    blocks, rows, d = terms.shape
    many = n_v // 2
    swapped = lax.all_to_all(
        terms.reshape(2, blocks // 2, rows, d), "vocab", 0, 0, axis_index_groups=pair_groups(n_v)
    )
    mine = (swapped[0] + swapped[1]).astype(jnp.bfloat16)
    mine = mine.reshape(many, blocks // 2 * rows // many, d)
    parts = lax.all_to_all(mine, "vocab", 0, 0, axis_index_groups=core_groups(n_v))
    total = jnp.sum(parts.astype(jnp.float32), axis=0).astype(jnp.bfloat16)
    return spread(total, many, core_groups(n_v))


def body(hidden, head_weight, teacher_logprobs, lengths, seq_weights):
    n_dp, n_v = lax.axis_size("dp"), lax.axis_size("vocab")
    me = lax.axis_index("dp")
    depth, width = head_weight.shape
    tok_rows = hidden.shape[0]
    deep = depth * GATHERED // 16
    gathered = lax.all_gather(head_weight[:deep], "dp", axis=0, tiled=True)
    pieces = ring_blocks(head_weight[deep:], n_dp)
    teacher = lax.all_to_all(teacher_logprobs, "vocab", split_axis=1, concat_axis=0, tiled=True)
    share = lax.all_to_all(hidden_share(hidden, n_dp, n_v), "dp", 0, 0)
    everyone = spread(share, n_v)

    rows = jnp.arange(tok_rows, dtype=jnp.int32)
    sequence = rows // SEQ_LEN
    position = rows % SEQ_LEN
    member = sequence[:, None] == jnp.arange(lengths.shape[0], dtype=jnp.int32)[None, :]
    row_length = jnp.sum(jnp.where(member, lengths[None, :], 0), axis=1)
    row_weight = jnp.sum(jnp.where(member, seq_weights[None, :], jnp.float32(0.0)), axis=1)
    weight = jnp.where(position < row_length, row_weight, jnp.float32(0.0)).reshape(1, tok_rows)

    features = hidden.reshape(tok_rows, n_dp, depth)
    first = features[:, :, :deep].reshape(tok_rows, n_dp * deep)
    logits = None
    for k in range(n_dp):
        feats = lax.dynamic_slice_in_dim(
            hidden, lax.rem(me + k, n_dp) * depth + deep, depth - deep, 1
        )
        term = jnp.dot(feats, pieces[k], preferred_element_type=jnp.float32)
        logits = term if logits is None else logits + term
    gathered, everyone, teacher, logits, weight, first = lax.optimization_barrier(
        (gathered, everyone, teacher, logits, weight, first)
    )
    logits = logits + jnp.dot(first, gathered, preferred_element_type=jnp.float32)
    stats = row_kernel(stats_kernel, (n_v, 3, tok_rows), jnp.float32, teacher, logits)
    every = lax.all_to_all(stats, "vocab", 0, 0)
    grad_logits = row_kernel(
        grads_kernel, logits.shape, jnp.bfloat16, every, weight, teacher, logits
    )

    everyone, grad_logits = lax.optimization_barrier((everyone, grad_logits))
    slices = everyone.transpose(1, 0, 2, 3).reshape(n_dp * tok_rows, depth)
    all_grads = lax.all_gather(grad_logits, "dp", axis=0, tiled=True)
    whole = sum_terms(hidden_terms(me, grad_logits, gathered, pieces), n_v)
    grad_head = lax.dot_general(
        slices, all_grads, (((0,), (0,)), ((), ())), preferred_element_type=jnp.float32
    ).astype(jnp.bfloat16)
    whole, grad_head = lax.optimization_barrier((whole, grad_head))
    summed = spread(whole, 2, pair_groups(n_v)).reshape(n_dp, tok_rows, depth)
    grad_hidden = jnp.concatenate([summed[k] for k in range(n_dp)], axis=1)
    return grad_hidden, grad_head


def solution(mesh):
    placed = (P("dp", None), P("dp", "vocab"), P(("dp", "vocab"), None), P("dp"), P("dp"))
    return jax.shard_map(
        body,
        mesh=mesh,
        in_specs=placed,
        out_specs=(P("dp", None), P("dp", "vocab")),
        check_vma=False,
    )
```

```python
import jax
import jax.numpy as jnp
from jax import lax
from jax.experimental import pallas as pl
from jax.experimental.pallas import tpu as pltpu
from jax.sharding import PartitionSpec as P

SEQ_LEN = 64
LOSS_SCALE = 32.0
GATHERED = 12
LANES = 128
VMEM = pl.BlockSpec(memory_space=pltpu.VMEM)
HBM = pl.BlockSpec(memory_space=pl.ANY)


def pair_groups(n):
    return [[2 * i, 2 * i + 1] for i in range(n // 2)]


def core_groups(n):
    return [[2 * i + c for i in range(n // 2)] for c in range(2)]


def spread(block, size, groups=None, axis="vocab"):
    copies = jnp.broadcast_to(block[None], (size,) + block.shape)
    return lax.all_to_all(copies, axis, 0, 0, axis_index_groups=groups)


def hidden_share(hidden, n_dp, n_v):
    rows, d = hidden.shape
    share = rows // n_v
    mine = lax.dynamic_slice_in_dim(hidden, lax.axis_index("vocab") * share, share, 0)
    return mine.reshape(share, n_dp, d // n_dp).transpose(1, 0, 2)


def ring_blocks(block, n):
    right = [(i, (i + 1) % n) for i in range(n)]
    left = [(i, (i - 1) % n) for i in range(n)]
    half = block.shape[0] // 2
    got = {0: block}
    up = down = block
    for step in range(1, n // 2):
        down, up = lax.ppermute(down, "dp", left), lax.ppermute(up, "dp", right)
        got[step], got[n - step] = down, up
    got[n // 2] = jnp.concatenate(
        [lax.ppermute(down[:half], "dp", left), lax.ppermute(up[half:], "dp", right)]
    )
    return [got[k] for k in range(n)]


def along_lanes(column, rows):
    return jnp.transpose(jnp.broadcast_to(column, (rows, LANES)))[:1]


def stats_kernel(teacher_ref, logits_ref, out_ref):
    rows = logits_ref.shape[0]
    logits = logits_ref[...]
    top = jnp.max(logits, axis=1, keepdims=True)
    shifted = logits - top
    expd = jnp.exp(shifted)
    total = jnp.sum(expd, axis=1, keepdims=True)
    gaps = expd * (shifted - teacher_ref[...].astype(jnp.float32))
    weighted = jnp.sum(gaps, axis=1, keepdims=True)
    stats = jnp.concatenate([along_lanes(v, rows) for v in (top, total, weighted)], axis=0)
    out_ref[...] = jnp.broadcast_to(stats[None], out_ref.shape)


def grads_kernel(every_ref, weight_ref, teacher_ref, logits_ref, out_ref):
    rows, width = logits_ref.shape
    tops, sums, weighteds = (every_ref[:, i, :] for i in range(3))
    top = jnp.max(tops, axis=0, keepdims=True)
    lower = tops - top
    scale = jnp.exp(lower)
    total = jnp.sum(sums * scale, axis=0, keepdims=True)
    weighted = jnp.sum(scale * (weighteds + lower * sums), axis=0, keepdims=True)
    factor = LOSS_SCALE * weight_ref[...] / total
    top, factor, centre = (
        jnp.transpose(jnp.broadcast_to(v, (LANES, rows))) for v in (top, factor, weighted / total)
    )
    for c in range(width // LANES):
        cols = pl.ds(c * LANES, LANES)
        shifted = logits_ref[:, cols] - top
        gap = shifted - teacher_ref[:, cols].astype(jnp.float32) - centre
        out_ref[:, cols] = (factor * jnp.exp(shifted) * gap).astype(jnp.bfloat16)


def terms_kernel(me_ref, grads_ref, gathered_ref, *refs):
    pieces, (out_ref, head, sems, piece_sems) = refs[:-4], refs[-4:]
    blocks, depth, _ = head.shape
    deep = depth - pieces[0].shape[0]
    places = [lax.rem(me_ref[0] + j, blocks) for j in range(blocks)]
    copies = [
        (
            pltpu.make_async_copy(
                piece, head.at[j, pl.ds(deep, depth - deep)], piece_sems.at[j]
            ),
            pltpu.make_async_copy(
                gathered_ref.at[pl.ds(pl.multiple_of(places[j] * deep, deep), deep)],
                head.at[j, pl.ds(0, deep)],
                sems.at[j],
            ),
        )
        for j, piece in enumerate(pieces)
    ]
    for pair in copies:
        for copy in pair:
            copy.start()
    grads = grads_ref[...]
    for j, pair in enumerate(copies):
        for copy in pair:
            copy.wait()
        out_ref[places[j]] = lax.dot_general(
            grads, head[j], (((1,), (1,)), ((), ())), preferred_element_type=jnp.float32
        )


def hidden_terms(me, grads, gathered, pieces):
    rows, width = grads.shape
    blocks = len(pieces)
    deep, rest = gathered.shape[0] // blocks, pieces[0].shape[0]
    d = blocks * (deep + rest)
    return pl.pallas_call(
        terms_kernel,
        out_shape=jax.ShapeDtypeStruct((blocks, rows, deep + rest), jnp.float32),
        in_specs=[pl.BlockSpec(memory_space=pltpu.SMEM), VMEM, HBM] + [HBM] * blocks,
        out_specs=VMEM,
        scratch_shapes=[
            pltpu.VMEM((blocks, deep + rest, width), gathered.dtype),
            pltpu.SemaphoreType.DMA((blocks,)),
            pltpu.SemaphoreType.DMA((blocks,)),
        ],
        compiler_params=pltpu.CompilerParams(vmem_limit_bytes=56 * 2**20),
        cost_estimate=pl.CostEstimate(
            flops=2 * rows * d * width, bytes_accessed=2 * d * width + 4 * rows * d, transcendentals=0
        ),
    )(me.reshape(1), grads, gathered, *pieces)


def halves_kernel(core_ref, kept_ref, got_ref, out_ref):
    some, _, depth = kept_ref.shape
    for half, ref in ((core_ref[0], kept_ref), (1 - core_ref[0], got_ref)):
        for i in range(some):
            at = pl.multiple_of((half * some + i) * depth, depth)
            out_ref[:, pl.ds(at, depth)] = ref[i]


def both_halves(kept, got):
    some, rows, depth = kept.shape
    core = lax.rem(lax.axis_index("vocab"), 2)
    return pl.pallas_call(
        halves_kernel,
        out_shape=jax.ShapeDtypeStruct((rows, 2 * some * depth), kept.dtype),
        in_specs=[pl.BlockSpec(memory_space=pltpu.SMEM), VMEM, VMEM],
        out_specs=VMEM,
        compiler_params=pltpu.CompilerParams(vmem_limit_bytes=16 * 2**20),
    )(core.reshape(1), kept, got)


def row_kernel(kernel, shape, dtype, *args):
    size = args[-1].size
    return pl.pallas_call(
        kernel,
        out_shape=jax.ShapeDtypeStruct(shape, dtype),
        in_specs=[VMEM] * len(args),
        out_specs=VMEM,
        compiler_params=pltpu.CompilerParams(vmem_limit_bytes=16 * 2**20),
        cost_estimate=pl.CostEstimate(flops=8 * size, bytes_accessed=8 * size, transcendentals=size),
    )(*args)


def sum_terms(terms, n_v):
    blocks, rows, d = terms.shape
    many = n_v // 2
    swapped = lax.all_to_all(
        terms.reshape(2, blocks // 2, rows, d), "vocab", 0, 0, axis_index_groups=pair_groups(n_v)
    )
    mine = (swapped[0] + swapped[1]).astype(jnp.bfloat16)
    mine = mine.reshape(many, blocks // 2 * rows // many, d)
    parts = lax.all_to_all(mine, "vocab", 0, 0, axis_index_groups=core_groups(n_v))
    total = jnp.sum(parts.astype(jnp.float32), axis=0).astype(jnp.bfloat16)
    return spread(total, many, core_groups(n_v))


def body(hidden, head_weight, teacher_logprobs, lengths, seq_weights):
    n_dp, n_v = lax.axis_size("dp"), lax.axis_size("vocab")
    me = lax.axis_index("dp")
    depth, width = head_weight.shape
    tok_rows = hidden.shape[0]
    deep = depth * GATHERED // 16
    gathered = lax.all_gather(head_weight[:deep], "dp", axis=0, tiled=True)
    pieces = ring_blocks(head_weight[deep:], n_dp)
    teacher = lax.all_to_all(teacher_logprobs, "vocab", split_axis=1, concat_axis=0, tiled=True)
    share = lax.all_to_all(hidden_share(hidden, n_dp, n_v), "dp", 0, 0)
    everyone = spread(share, n_v)

    rows = jnp.arange(tok_rows, dtype=jnp.int32)
    sequence = rows // SEQ_LEN
    position = rows % SEQ_LEN
    member = sequence[:, None] == jnp.arange(lengths.shape[0], dtype=jnp.int32)[None, :]
    row_length = jnp.sum(jnp.where(member, lengths[None, :], 0), axis=1)
    row_weight = jnp.sum(jnp.where(member, seq_weights[None, :], jnp.float32(0.0)), axis=1)
    weight = jnp.where(position < row_length, row_weight, jnp.float32(0.0)).reshape(1, tok_rows)

    features = hidden.reshape(tok_rows, n_dp, depth)
    first = features[:, :, :deep].reshape(tok_rows, n_dp * deep)
    logits = None
    for k in range(n_dp):
        feats = lax.dynamic_slice_in_dim(
            hidden, lax.rem(me + k, n_dp) * depth + deep, depth - deep, 1
        )
        term = jnp.dot(feats, pieces[k], preferred_element_type=jnp.float32)
        logits = term if logits is None else logits + term
    gathered, everyone, teacher, logits, weight, first = lax.optimization_barrier(
        (gathered, everyone, teacher, logits, weight, first)
    )
    logits = logits + jnp.dot(first, gathered, preferred_element_type=jnp.float32)
    stats = row_kernel(stats_kernel, (n_v, 3, tok_rows), jnp.float32, teacher, logits)
    every = lax.all_to_all(stats, "vocab", 0, 0)
    grad_logits = row_kernel(
        grads_kernel, logits.shape, jnp.bfloat16, every, weight, teacher, logits
    )

    everyone, grad_logits = lax.optimization_barrier((everyone, grad_logits))
    slices = everyone.transpose(1, 0, 2, 3).reshape(n_dp * tok_rows, depth)
    all_grads = lax.all_gather(grad_logits, "dp", axis=0, tiled=True)
    whole = sum_terms(hidden_terms(me, grad_logits, gathered, pieces), n_v)
    grad_head = lax.dot_general(
        slices, all_grads, (((0,), (0,)), ((), ())), preferred_element_type=jnp.float32
    ).astype(jnp.bfloat16)
    whole, grad_head = lax.optimization_barrier((whole, grad_head))
    kept = whole.reshape(n_dp // 2, tok_rows, depth)
    got = lax.ppermute(kept, "vocab", [(i, i ^ 1) for i in range(n_v)])
    grad_hidden = both_halves(kept, got)
    return grad_hidden, grad_head


def solution(mesh):
    placed = (P("dp", None), P("dp", "vocab"), P(("dp", "vocab"), None), P("dp"), P("dp"))
    return jax.shard_map(
        body,
        mesh=mesh,
        in_specs=placed,
        out_specs=(P("dp", None), P("dp", "vocab")),
        check_vma=False,
    )
```

```python
import jax
import jax.numpy as jnp
from jax import lax
from jax.experimental import pallas as pl
from jax.experimental.pallas import tpu as pltpu
from jax.sharding import PartitionSpec as P

SEQ_LEN = 64
LOSS_SCALE = 32.0
GATHERED = 11
LANES = 128
VMEM = pl.BlockSpec(memory_space=pltpu.VMEM)
HBM = pl.BlockSpec(memory_space=pl.ANY)


def pair_groups(n):
    return [[2 * i, 2 * i + 1] for i in range(n // 2)]


def core_groups(n):
    return [[2 * i + c for i in range(n // 2)] for c in range(2)]


def spread(block, size, groups=None, axis="vocab"):
    copies = jnp.broadcast_to(block[None], (size,) + block.shape)
    return lax.all_to_all(copies, axis, 0, 0, axis_index_groups=groups)


def hidden_share(hidden, n_dp, n_v):
    rows, d = hidden.shape
    share = rows // n_v
    mine = lax.dynamic_slice_in_dim(hidden, lax.axis_index("vocab") * share, share, 0)
    return mine.reshape(share, n_dp, d // n_dp).transpose(1, 0, 2)


def ring_blocks(block, n, beside):
    right = [(i, (i + 1) % n) for i in range(n)]
    left = [(i, (i - 1) % n) for i in range(n)]
    half = block.shape[0] // 2
    got = {0: block}
    up = down = block
    for step in range(1, n // 2):
        if step == 3:
            down, up, beside = lax.optimization_barrier((down, up, beside))
        down, up = lax.ppermute(down, "dp", left), lax.ppermute(up, "dp", right)
        got[step], got[n - step] = down, up
    got[n // 2] = jnp.concatenate(
        [lax.ppermute(down[:half], "dp", left), lax.ppermute(up[half:], "dp", right)]
    )
    return [got[k] for k in range(n)], beside


def along_lanes(column, rows):
    return jnp.transpose(jnp.broadcast_to(column, (rows, LANES)))[:1]


def stats_kernel(teacher_ref, logits_ref, out_ref):
    rows = logits_ref.shape[0]
    logits = logits_ref[...]
    top = jnp.max(logits, axis=1, keepdims=True)
    shifted = logits - top
    expd = jnp.exp(shifted)
    total = jnp.sum(expd, axis=1, keepdims=True)
    gaps = expd * (shifted - teacher_ref[...].astype(jnp.float32))
    weighted = jnp.sum(gaps, axis=1, keepdims=True)
    stats = jnp.concatenate([along_lanes(v, rows) for v in (top, total, weighted)], axis=0)
    out_ref[...] = jnp.broadcast_to(stats[None], out_ref.shape)


def grads_kernel(every_ref, weight_ref, teacher_ref, logits_ref, out_ref):
    rows, width = logits_ref.shape
    tops, sums, weighteds = (every_ref[:, i, :] for i in range(3))
    top = jnp.max(tops, axis=0, keepdims=True)
    lower = tops - top
    scale = jnp.exp(lower)
    total = jnp.sum(sums * scale, axis=0, keepdims=True)
    weighted = jnp.sum(scale * (weighteds + lower * sums), axis=0, keepdims=True)
    factor = LOSS_SCALE * weight_ref[...] / total
    top, factor, centre = (
        jnp.transpose(jnp.broadcast_to(v, (LANES, rows))) for v in (top, factor, weighted / total)
    )
    for c in range(width // LANES):
        cols = pl.ds(c * LANES, LANES)
        shifted = logits_ref[:, cols] - top
        gap = shifted - teacher_ref[:, cols].astype(jnp.float32) - centre
        out_ref[:, cols] = (factor * jnp.exp(shifted) * gap).astype(jnp.bfloat16)


def terms_kernel(me_ref, grads_ref, gathered_ref, *refs):
    pieces, (out_ref, head, sems, piece_sems) = refs[:-4], refs[-4:]
    blocks, depth, _ = head.shape
    deep = depth - pieces[0].shape[0]
    places = [lax.rem(me_ref[0] + j, blocks) for j in range(blocks)]
    copies = [
        (
            pltpu.make_async_copy(
                piece, head.at[j, pl.ds(deep, depth - deep)], piece_sems.at[j]
            ),
            pltpu.make_async_copy(
                gathered_ref.at[pl.ds(pl.multiple_of(places[j] * deep, deep), deep)],
                head.at[j, pl.ds(0, deep)],
                sems.at[j],
            ),
        )
        for j, piece in enumerate(pieces)
    ]
    for pair in copies:
        for copy in pair:
            copy.start()
    grads = grads_ref[...]
    for j, pair in enumerate(copies):
        for copy in pair:
            copy.wait()
        out_ref[places[j]] = lax.dot_general(
            grads, head[j], (((1,), (1,)), ((), ())), preferred_element_type=jnp.float32
        )


def hidden_terms(me, grads, gathered, pieces):
    rows, width = grads.shape
    blocks = len(pieces)
    deep, rest = gathered.shape[0] // blocks, pieces[0].shape[0]
    d = blocks * (deep + rest)
    return pl.pallas_call(
        terms_kernel,
        out_shape=jax.ShapeDtypeStruct((blocks, rows, deep + rest), jnp.float32),
        in_specs=[pl.BlockSpec(memory_space=pltpu.SMEM), VMEM, HBM] + [HBM] * blocks,
        out_specs=VMEM,
        scratch_shapes=[
            pltpu.VMEM((blocks, deep + rest, width), gathered.dtype),
            pltpu.SemaphoreType.DMA((blocks,)),
            pltpu.SemaphoreType.DMA((blocks,)),
        ],
        compiler_params=pltpu.CompilerParams(vmem_limit_bytes=56 * 2**20),
        cost_estimate=pl.CostEstimate(
            flops=2 * rows * d * width, bytes_accessed=2 * d * width + 4 * rows * d, transcendentals=0
        ),
    )(me.reshape(1), grads, gathered, *pieces)


def halves_kernel(core_ref, kept_ref, got_ref, out_ref):
    some, _, depth = kept_ref.shape
    for half, ref in ((core_ref[0], kept_ref), (1 - core_ref[0], got_ref)):
        for i in range(some):
            at = pl.multiple_of((half * some + i) * depth, depth)
            out_ref[:, pl.ds(at, depth)] = ref[i]


def both_halves(kept, got):
    some, rows, depth = kept.shape
    core = lax.rem(lax.axis_index("vocab"), 2)
    return pl.pallas_call(
        halves_kernel,
        out_shape=jax.ShapeDtypeStruct((rows, 2 * some * depth), kept.dtype),
        in_specs=[pl.BlockSpec(memory_space=pltpu.SMEM), VMEM, VMEM],
        out_specs=VMEM,
        compiler_params=pltpu.CompilerParams(vmem_limit_bytes=16 * 2**20),
    )(core.reshape(1), kept, got)


def row_kernel(kernel, shape, dtype, *args):
    size = args[-1].size
    return pl.pallas_call(
        kernel,
        out_shape=jax.ShapeDtypeStruct(shape, dtype),
        in_specs=[VMEM] * len(args),
        out_specs=VMEM,
        compiler_params=pltpu.CompilerParams(vmem_limit_bytes=16 * 2**20),
        cost_estimate=pl.CostEstimate(flops=8 * size, bytes_accessed=8 * size, transcendentals=size),
    )(*args)


def sum_terms(terms, n_v):
    blocks, rows, d = terms.shape
    many = n_v // 2
    swapped = lax.all_to_all(
        terms.reshape(2, blocks // 2, rows, d), "vocab", 0, 0, axis_index_groups=pair_groups(n_v)
    )
    mine = (swapped[0] + swapped[1]).astype(jnp.bfloat16)
    mine = mine.reshape(many, blocks // 2 * rows // many, d)
    parts = lax.all_to_all(mine, "vocab", 0, 0, axis_index_groups=core_groups(n_v))
    total = jnp.sum(parts.astype(jnp.float32), axis=0).astype(jnp.bfloat16)
    return spread(total, many, core_groups(n_v))


def body(hidden, head_weight, teacher_logprobs, lengths, seq_weights):
    n_dp, n_v = lax.axis_size("dp"), lax.axis_size("vocab")
    me = lax.axis_index("dp")
    depth, width = head_weight.shape
    tok_rows = hidden.shape[0]
    deep = depth * GATHERED // 16
    gathered = lax.all_gather(head_weight[:deep], "dp", axis=0, tiled=True)
    teacher = lax.all_to_all(teacher_logprobs, "vocab", split_axis=1, concat_axis=0, tiled=True)
    pieces, teacher = ring_blocks(head_weight[deep:], n_dp, teacher)
    share = lax.all_to_all(hidden_share(hidden, n_dp, n_v), "dp", 0, 0)
    everyone = spread(share, n_v)

    rows = jnp.arange(tok_rows, dtype=jnp.int32)
    sequence = rows // SEQ_LEN
    position = rows % SEQ_LEN
    member = sequence[:, None] == jnp.arange(lengths.shape[0], dtype=jnp.int32)[None, :]
    row_length = jnp.sum(jnp.where(member, lengths[None, :], 0), axis=1)
    row_weight = jnp.sum(jnp.where(member, seq_weights[None, :], jnp.float32(0.0)), axis=1)
    weight = jnp.where(position < row_length, row_weight, jnp.float32(0.0)).reshape(1, tok_rows)

    features = hidden.reshape(tok_rows, n_dp, depth)
    first = features[:, :, :deep].reshape(tok_rows, n_dp * deep)
    logits = None
    for k in range(n_dp):
        feats = lax.dynamic_slice_in_dim(
            hidden, lax.rem(me + k, n_dp) * depth + deep, depth - deep, 1
        )
        term = jnp.dot(feats, pieces[k], preferred_element_type=jnp.float32)
        logits = term if logits is None else logits + term
    gathered, everyone, teacher, logits, weight, first = lax.optimization_barrier(
        (gathered, everyone, teacher, logits, weight, first)
    )
    logits = logits + jnp.dot(first, gathered, preferred_element_type=jnp.float32)
    stats = row_kernel(stats_kernel, (n_v, 3, tok_rows), jnp.float32, teacher, logits)
    every = lax.all_to_all(stats, "vocab", 0, 0)
    grad_logits = row_kernel(
        grads_kernel, logits.shape, jnp.bfloat16, every, weight, teacher, logits
    )

    everyone, grad_logits = lax.optimization_barrier((everyone, grad_logits))
    slices = everyone.transpose(1, 0, 2, 3).reshape(n_dp * tok_rows, depth)
    all_grads = lax.all_gather(grad_logits, "dp", axis=0, tiled=True)
    whole = sum_terms(hidden_terms(me, grad_logits, gathered, pieces), n_v)
    grad_head = lax.dot_general(
        slices, all_grads, (((0,), (0,)), ((), ())), preferred_element_type=jnp.float32
    ).astype(jnp.bfloat16)
    whole, grad_head = lax.optimization_barrier((whole, grad_head))
    kept = whole.reshape(n_dp // 2, tok_rows, depth)
    got = lax.ppermute(kept, "vocab", [(i, i ^ 1) for i in range(n_v)])
    grad_hidden = both_halves(kept, got)
    return grad_hidden, grad_head


def solution(mesh):
    placed = (P("dp", None), P("dp", "vocab"), P(("dp", "vocab"), None), P("dp"), P("dp"))
    return jax.shard_map(
        body,
        mesh=mesh,
        in_specs=placed,
        out_specs=(P("dp", None), P("dp", "vocab")),
        check_vma=False,
    )
```

```python
import jax
import jax.numpy as jnp
from jax import lax
from jax.experimental import pallas as pl
from jax.experimental.pallas import tpu as pltpu
from jax.sharding import PartitionSpec as P

SEQ_LEN = 64
LOSS_SCALE = 32.0
GATHERED = 11
LANES = 128
VMEM = pl.BlockSpec(memory_space=pltpu.VMEM)
HBM = pl.BlockSpec(memory_space=pl.ANY)


def core_groups(n):
    return [[2 * i + c for i in range(n // 2)] for c in range(2)]


def spread(block, size, groups=None, axis="vocab"):
    copies = jnp.broadcast_to(block[None], (size,) + block.shape)
    return lax.all_to_all(copies, axis, 0, 0, axis_index_groups=groups)


def hidden_share(hidden, n_dp, n_v):
    rows, d = hidden.shape
    share = rows // n_v
    mine = lax.dynamic_slice_in_dim(hidden, lax.axis_index("vocab") * share, share, 0)
    return mine.reshape(share, n_dp, d // n_dp).transpose(1, 0, 2)


def ring_blocks(block, n, beside):
    right = [(i, (i + 1) % n) for i in range(n)]
    left = [(i, (i - 1) % n) for i in range(n)]
    half = block.shape[0] // 2
    got = {0: block}
    up = down = block
    for step in range(1, n // 2):
        if step == 3:
            down, up, beside = lax.optimization_barrier((down, up, beside))
        down, up = lax.ppermute(down, "dp", left), lax.ppermute(up, "dp", right)
        got[step], got[n - step] = down, up
    got[n // 2] = jnp.concatenate(
        [lax.ppermute(down[:half], "dp", left), lax.ppermute(up[half:], "dp", right)]
    )
    return [got[k] for k in range(n)], beside


def along_lanes(column, rows):
    return jnp.transpose(jnp.broadcast_to(column, (rows, LANES)))[:1]


def stats_kernel(teacher_ref, logits_ref, out_ref):
    rows = logits_ref.shape[0]
    logits = logits_ref[...]
    top = jnp.max(logits, axis=1, keepdims=True)
    shifted = logits - top
    expd = jnp.exp(shifted)
    total = jnp.sum(expd, axis=1, keepdims=True)
    gaps = expd * (shifted - teacher_ref[...].astype(jnp.float32))
    weighted = jnp.sum(gaps, axis=1, keepdims=True)
    stats = jnp.concatenate([along_lanes(v, rows) for v in (top, total, weighted)], axis=0)
    out_ref[...] = jnp.broadcast_to(stats[None], out_ref.shape)


def grads_kernel(every_ref, weight_ref, teacher_ref, logits_ref, out_ref):
    rows, width = logits_ref.shape
    tops, sums, weighteds = (every_ref[:, i, :] for i in range(3))
    top = jnp.max(tops, axis=0, keepdims=True)
    lower = tops - top
    scale = jnp.exp(lower)
    total = jnp.sum(sums * scale, axis=0, keepdims=True)
    weighted = jnp.sum(scale * (weighteds + lower * sums), axis=0, keepdims=True)
    factor = LOSS_SCALE * weight_ref[...] / total
    top, factor, centre = (
        jnp.transpose(jnp.broadcast_to(v, (LANES, rows))) for v in (top, factor, weighted / total)
    )
    for c in range(width // LANES):
        cols = pl.ds(c * LANES, LANES)
        shifted = logits_ref[:, cols] - top
        gap = shifted - teacher_ref[:, cols].astype(jnp.float32) - centre
        out_ref[:, cols] = (factor * jnp.exp(shifted) * gap).astype(jnp.bfloat16)


def terms_kernel(place_ref, grads_ref, gathered_ref, *refs):
    pieces, (kept_ref, sent_ref, head, sems, piece_sems) = refs[:-5], refs[-5:]
    blocks, depth, _ = head.shape
    deep = depth - pieces[0].shape[0]
    places = [lax.rem(place_ref[0] + j, blocks) for j in range(blocks)]
    some = blocks // 2
    copies = [
        (
            pltpu.make_async_copy(
                piece, head.at[j, pl.ds(deep, depth - deep)], piece_sems.at[j]
            ),
            pltpu.make_async_copy(
                gathered_ref.at[pl.ds(pl.multiple_of(places[j] * deep, deep), deep)],
                head.at[j, pl.ds(0, deep)],
                sems.at[j],
            ),
        )
        for j, piece in enumerate(pieces)
    ]
    for pair in copies:
        for copy in pair:
            copy.start()
    grads = grads_ref[...]
    for j, pair in enumerate(copies):
        for copy in pair:
            copy.wait()
        term = lax.dot_general(
            grads, head[j], (((1,), (1,)), ((), ())), preferred_element_type=jnp.float32
        )
        place = lax.rem(places[j], some)
        mine = (places[j] >= some) == (place_ref[1] == 1)

        @pl.when(mine)
        def _():
            kept_ref[place] = term

        @pl.when(jnp.logical_not(mine))
        def _():
            sent_ref[place] = term


def hidden_terms(me, core, grads, gathered, pieces):
    rows, width = grads.shape
    blocks = len(pieces)
    deep, rest = gathered.shape[0] // blocks, pieces[0].shape[0]
    d = blocks * (deep + rest)
    return pl.pallas_call(
        terms_kernel,
        out_shape=(jax.ShapeDtypeStruct((blocks // 2, rows, deep + rest), jnp.float32),) * 2,
        in_specs=[pl.BlockSpec(memory_space=pltpu.SMEM), VMEM, HBM] + [HBM] * blocks,
        out_specs=(VMEM, VMEM),
        scratch_shapes=[
            pltpu.VMEM((blocks, deep + rest, width), gathered.dtype),
            pltpu.SemaphoreType.DMA((blocks,)),
            pltpu.SemaphoreType.DMA((blocks,)),
        ],
        compiler_params=pltpu.CompilerParams(vmem_limit_bytes=56 * 2**20),
        cost_estimate=pl.CostEstimate(
            flops=2 * rows * d * width, bytes_accessed=2 * d * width + 4 * rows * d, transcendentals=0
        ),
    )(jnp.stack([me, core]), grads, gathered, *pieces)


def halves_kernel(core_ref, kept_ref, got_ref, out_ref):
    some, _, depth = kept_ref.shape
    for half, ref in ((core_ref[0], kept_ref), (1 - core_ref[0], got_ref)):
        for i in range(some):
            at = pl.multiple_of((half * some + i) * depth, depth)
            out_ref[:, pl.ds(at, depth)] = ref[i]


def both_halves(kept, got):
    some, rows, depth = kept.shape
    core = lax.rem(lax.axis_index("vocab"), 2)
    return pl.pallas_call(
        halves_kernel,
        out_shape=jax.ShapeDtypeStruct((rows, 2 * some * depth), kept.dtype),
        in_specs=[pl.BlockSpec(memory_space=pltpu.SMEM), VMEM, VMEM],
        out_specs=VMEM,
        compiler_params=pltpu.CompilerParams(vmem_limit_bytes=16 * 2**20),
    )(core.reshape(1), kept, got)


def row_kernel(kernel, shape, dtype, *args):
    size = args[-1].size
    return pl.pallas_call(
        kernel,
        out_shape=jax.ShapeDtypeStruct(shape, dtype),
        in_specs=[VMEM] * len(args),
        out_specs=VMEM,
        compiler_params=pltpu.CompilerParams(vmem_limit_bytes=16 * 2**20),
        cost_estimate=pl.CostEstimate(flops=8 * size, bytes_accessed=8 * size, transcendentals=size),
    )(*args)


def sum_terms(kept, sent, n_v):
    blocks, rows, d = kept.shape
    many = n_v // 2
    got = lax.ppermute(sent, "vocab", [(i, i ^ 1) for i in range(n_v)])
    mine = (kept + got).astype(jnp.bfloat16).reshape(many, blocks * rows // many, d)
    parts = lax.all_to_all(mine, "vocab", 0, 0, axis_index_groups=core_groups(n_v))
    total = jnp.sum(parts.astype(jnp.float32), axis=0).astype(jnp.bfloat16)
    return spread(total, many, core_groups(n_v))


def body(hidden, head_weight, teacher_logprobs, lengths, seq_weights):
    n_dp, n_v = lax.axis_size("dp"), lax.axis_size("vocab")
    me = lax.axis_index("dp")
    depth, width = head_weight.shape
    tok_rows = hidden.shape[0]
    deep = depth * GATHERED // 16
    gathered = lax.all_gather(head_weight[:deep], "dp", axis=0, tiled=True)
    teacher = lax.all_to_all(teacher_logprobs, "vocab", split_axis=1, concat_axis=0, tiled=True)
    pieces, teacher = ring_blocks(head_weight[deep:], n_dp, teacher)
    share = lax.all_to_all(hidden_share(hidden, n_dp, n_v), "dp", 0, 0)
    everyone = spread(share, n_v)

    rows = jnp.arange(tok_rows, dtype=jnp.int32)
    sequence = rows // SEQ_LEN
    position = rows % SEQ_LEN
    member = sequence[:, None] == jnp.arange(lengths.shape[0], dtype=jnp.int32)[None, :]
    row_length = jnp.sum(jnp.where(member, lengths[None, :], 0), axis=1)
    row_weight = jnp.sum(jnp.where(member, seq_weights[None, :], jnp.float32(0.0)), axis=1)
    weight = jnp.where(position < row_length, row_weight, jnp.float32(0.0)).reshape(1, tok_rows)

    features = hidden.reshape(tok_rows, n_dp, depth)
    first = features[:, :, :deep].reshape(tok_rows, n_dp * deep)
    logits = None
    for k in range(n_dp):
        feats = lax.dynamic_slice_in_dim(
            hidden, lax.rem(me + k, n_dp) * depth + deep, depth - deep, 1
        )
        term = jnp.dot(feats, pieces[k], preferred_element_type=jnp.float32)
        logits = term if logits is None else logits + term
    gathered, everyone, teacher, logits, weight, first = lax.optimization_barrier(
        (gathered, everyone, teacher, logits, weight, first)
    )
    logits = logits + jnp.dot(first, gathered, preferred_element_type=jnp.float32)
    stats = row_kernel(stats_kernel, (n_v, 3, tok_rows), jnp.float32, teacher, logits)
    every = lax.all_to_all(stats, "vocab", 0, 0)
    grad_logits = row_kernel(
        grads_kernel, logits.shape, jnp.bfloat16, every, weight, teacher, logits
    )

    everyone, grad_logits = lax.optimization_barrier((everyone, grad_logits))
    slices = everyone.transpose(1, 0, 2, 3).reshape(n_dp * tok_rows, depth)
    all_grads = lax.all_gather(grad_logits, "dp", axis=0, tiled=True)
    core = lax.rem(lax.axis_index("vocab"), 2)
    kept, sent = hidden_terms(me, core, grad_logits, gathered, pieces)
    whole = sum_terms(kept, sent, n_v)
    grad_head = lax.dot_general(
        slices, all_grads, (((0,), (0,)), ((), ())), preferred_element_type=jnp.float32
    ).astype(jnp.bfloat16)
    whole, grad_head = lax.optimization_barrier((whole, grad_head))
    kept = whole.reshape(n_dp // 2, tok_rows, depth)
    got = lax.ppermute(kept, "vocab", [(i, i ^ 1) for i in range(n_v)])
    grad_hidden = both_halves(kept, got)
    return grad_hidden, grad_head


def solution(mesh):
    placed = (P("dp", None), P("dp", "vocab"), P(("dp", "vocab"), None), P("dp"), P("dp"))
    return jax.shard_map(
        body,
        mesh=mesh,
        in_specs=placed,
        out_specs=(P("dp", None), P("dp", "vocab")),
        check_vma=False,
    )
```
